32 devices in a mesh: groups: 2 (over y), expert: 4 (over z), tensor: 2 (over x), pair: 2 (over core).
Axes of the slice: x: 2, y: 2, z: 4, core: 2. Of those that a mesh axis runs over, the one named last changes fastest.
Arguments:
- hidden: bfloat16 [384, 3584], P(('groups', 'expert'), ('tensor', 'pair')), parts along dimension 0, may hold values from -6 to 6
- routes: int32 [384, 8], P(('groups', 'expert')), parts along dimension 0, may hold values from 0 to 31, all different within a row; in each aligned block of 48 rows (0 to 47, 48 to 95, ...) at most 18 rows name the same one
- w_router: bfloat16 [3584, 32], P(('tensor', 'pair')), may hold values from -0.09375 to 0.09375
- w_gate: bfloat16 [32, 3584, 1024], P('expert', None, ('tensor', 'pair')), may hold values from -0.09375 to 0.09375
- w_up: bfloat16 [32, 3584, 1024], P('expert', None, ('tensor', 'pair')), may hold values from -0.09375 to 0.09375
- w_down: bfloat16 [32, 1024, 3584], P('expert', ('tensor', 'pair')), may hold values from -0.1875 to 0.1875
Outputs:
- layer_out: bfloat16 [384, 3584], P(('groups', 'expert'), ('tensor', 'pair')), parts along dimension 0
The draws below stay inside these ranges and needn't reach their ends.
There are 2 independent parts, one for each index of `groups`. The reference program is written for one: setup_inputs(seed, part) draws one part's arguments, and reference() takes and returns one part's arrays. A program takes and returns all parts, laid end to end along the dimension named above; an argument that names none is the same for every part. Nothing has to cross between parts.
Inputs may be any that keep to these rules, and one draw needn't show every extreme that they name: `routes`: each row names 8 different experts. Among the 48 rows of one device (aligned blocks) no expert is named by more than 18 rows, a bound that some block reaches.
All inputs are finite; a program needn't handle non-finite values.
Results may differ from the reference program's by a relative error of at most 0.0075.
Values may be sent and summed in bfloat16 or wider, within the bound.
A program may use at most 192 MiB of HBM per device.

```python
import math
import jax
import jax.numpy as jnp
import numpy as np
from jax import lax

D = 3584
FF = 1024
E = 32
TOP = 8
CAP = 18
ROWS_DEV = 48
ROWS = 192
N_EXPERT = 4
N_TENSOR = 2
N_PAIR = 2


def levels(key, shape, cuts, least, top_value):
    def one(position, parts):
        heights = jax.random.uniform(jax.random.fold_in(jax.random.fold_in(key, 6), position), (parts,), jnp.float32, least / len(cuts), top_value / len(cuts))
        return jnp.repeat(jnp.exp(heights), shape[position] // parts).reshape((-1,) + (1,) * (len(shape) - position - 1))

    level = one(*cuts[0])
    for cut in cuts[1:]:
        level = level * one(*cut)
    return level


def shared_out(rng, own, number, rows, count, top, limit, skew):
    sequence = jax.random.permutation(rng, count)
    heavy_load, usual = load_shares(count, rows * top, limit, skew, True), load_shares(count, rows * top, limit, skew, False)
    places = jnp.arange(count)

    def named(sizes, rotation):
        used = int((sizes > 0).sum())
        fixed = max(1, used // 4)
        shifted = fixed + (places - fixed + rotation * (used - fixed)) % max(1, count - fixed)
        return jnp.zeros((count,), jnp.int32).at[sequence[jnp.where(places < fixed, places, shifted)]].set(jnp.asarray(sizes, jnp.int32))

    sizes = jnp.where(number % 4 == 0, named(heavy_load, number // 4), named(usual, number - number // 4 - 1))
    mixed = jax.random.permutation(jax.random.fold_in(own, 3), count)
    giver, sink = mixed[0:count // 2 * 2:2], mixed[1:count // 2 * 2:2]
    slack = jnp.minimum(sizes[giver] - 1, limit - sizes[sink]) // 2
    slack = jnp.where((giver == sequence[0]) | (sink == sequence[0]) | (sizes[sink] == 0), 0, jnp.maximum(slack, 0))
    shifted = jax.random.randint(jax.random.fold_in(own, 4), (count // 2,), 0, 1 << 20) % (slack + 1)
    sizes = sizes.at[giver].add(-shifted).at[sink].add(shifted)
    items = jnp.searchsorted(jnp.cumsum(sizes), jnp.arange(rows * top), side="right").astype(jnp.int32)
    table = items.reshape(top, rows).T
    table = table[jax.random.permutation(jax.random.fold_in(own, 1), rows)]
    rotation = jax.random.randint(jax.random.fold_in(own, 2), (rows, 1), 0, top)
    return jnp.take_along_axis(table, (jnp.arange(top)[None, :] + rotation) % top, axis=1)


def load_shares(count, total, reach, skew, full):
    loads = [(1 << 20) // math.isqrt(standing ** skew) + 1 for standing in range(1, count + 1)]
    largest = reach if full else min(reach, max(-(-total // count), total * loads[0] // sum(loads)))
    least = 1 if total - largest >= count - 1 else 0
    holding, spare = [largest] + [least] * (count - 1), total - largest - least * (count - 1)
    while spare > 0:
        movable = [i for i in range(1, count) if holding[i] < largest] or [i for i in range(1, count) if holding[i] < reach]
        whole, left = sum([loads[i] for i in movable]), spare
        for i in movable:
            more = min(reach - holding[i], max(1, left * loads[i] // whole), spare)
            holding[i] = holding[i] + more
            spare = spare - more
    return np.array(holding)


def centred(rng, dims, spread, bound, split=(), held_as=jnp.bfloat16):
    loudness = levels(rng, dims, split, -0.22, 0.18) if split else 1.0
    drawn = jax.random.normal(rng, dims, jnp.float32) * spread * loudness
    return jnp.minimum(jnp.maximum(drawn, -bound), bound).astype(held_as)


def setup_inputs(seed: int = 0, part: int = 0) -> dict:
    keys = jax.random.split(jax.random.key(seed), 7)
    part_keys = jax.random.split(jax.random.fold_in(keys[6], part), 7)
    hidden = centred(part_keys[0], (ROWS, D), 1.0, 6.0, ((0, 4), (1, 4)))
    routes_keys = jax.random.split(jax.random.fold_in(part_keys[1], 1), ROWS // ROWS_DEV)
    routes_turns = jax.random.permutation(jax.random.fold_in(part_keys[1], 3), ROWS // ROWS_DEV)
    routes = jax.vmap(lambda own, number: shared_out(jax.random.fold_in(part_keys[1], 2), own, number, ROWS_DEV, E, TOP, CAP, 2))(routes_keys, routes_turns).reshape((ROWS, TOP))
    w_router = centred(keys[2], (D, E), D ** -0.5, 0.09375, ((0, 4),))
    w_gate = centred(keys[3], (E, D, FF), D ** -0.5, 0.09375, ((0, 4), (2, 4)))
    w_up = centred(keys[4], (E, D, FF), D ** -0.5, 0.09375, ((0, 4), (2, 4)))
    w_down = centred(keys[5], (E, FF, D), FF ** -0.5, 0.1875, ((0, 4), (1, 4)))
    return dict(hidden=hidden, routes=routes, w_router=w_router, w_gate=w_gate, w_up=w_up, w_down=w_down)


route_scale = 2.5


def expert_apply(operands):
    expert_input, gate_matrix, up_matrix, down_matrix = operands
    groups_count = N_TENSOR * N_PAIR
    block_units = FF // groups_count
    gate_act = jnp.dot(expert_input, gate_matrix, preferred_element_type=jnp.float32)
    up_act = jnp.dot(expert_input, up_matrix, preferred_element_type=jnp.float32)
    act = (jax.nn.silu(gate_act) * up_act).astype(jnp.bfloat16)
    pieces = act.reshape(act.shape[0], groups_count, block_units).astype(jnp.float32)
    down_pieces = down_matrix.reshape(groups_count, block_units, D).astype(jnp.float32)
    partial_value = jnp.einsum('mjf,jfd->jmd', pieces, down_pieces)
    rounded = lax.optimization_barrier(partial_value.astype(jnp.bfloat16))
    return jnp.sum(rounded.astype(jnp.float32), axis=0).astype(jnp.bfloat16)


def reference(hidden, routes, w_router, w_gate, w_up, w_down):
    blocks = N_EXPERT
    assign = ROWS_DEV * TOP
    logits = jnp.dot(hidden, w_router, preferred_element_type=jnp.float32)
    scores = jax.nn.sigmoid(logits)
    chosen = jnp.take_along_axis(scores, routes, axis=1)
    gate_values = (route_scale * chosen / jnp.sum(chosen, axis=1, keepdims=True)).astype(jnp.bfloat16)
    flat_routes = routes.reshape(blocks, assign)
    onehot = (flat_routes[:, :, None] == jnp.arange(E, dtype=jnp.int32)[None, None, :]).astype(jnp.int32)
    running = jnp.cumsum(onehot, axis=1) - 1
    slot_index = jnp.sum(running * onehot, axis=2).astype(jnp.int32)
    target = (flat_routes * CAP + slot_index).astype(jnp.int32)
    source = hidden.reshape(blocks, ROWS_DEV, D)
    picked = jnp.repeat(source, TOP, axis=1)
    block_index = jnp.arange(blocks, dtype=jnp.int32)[:, None]
    outbound = jnp.zeros((blocks, E * CAP, D), jnp.bfloat16).at[block_index, target].set(picked)
    per_expert = outbound.reshape(blocks, E, CAP, D).transpose(1, 0, 2, 3).reshape(E, blocks * CAP, D)
    outputs = lax.map(expert_apply, (per_expert, w_gate, w_up, w_down))
    slot_values = outputs.reshape(E, blocks, CAP, D).transpose(1, 0, 2, 3).reshape(blocks, E * CAP, D)
    fetched = slot_values[block_index, target]
    weighted = fetched.astype(jnp.float32).reshape(blocks * ROWS_DEV, TOP, D) * gate_values.astype(jnp.float32)[:, :, None]
    layer_out = hidden.astype(jnp.float32) + jnp.sum(weighted, axis=1)
    return layer_out.astype(jnp.bfloat16)
```

```python
import functools

import jax
import jax.numpy as jnp
from jax import lax
from jax.experimental import pallas as pl
from jax.experimental.pallas import tpu as pltpu
from jax.sharding import PartitionSpec as P

CAP = 18


route_scale = 2.5


def experts_apply(received, w_gate, w_up, w_down):
    gate_act = jnp.einsum("ecsd,edf->ecsf", received, w_gate, preferred_element_type=jnp.float32)
    up_act = jnp.einsum("ecsd,edf->ecsf", received, w_up, preferred_element_type=jnp.float32)
    hidden_act = (jax.nn.silu(gate_act) * up_act).astype(jnp.bfloat16)
    down_act = jnp.einsum("ecsf,efd->ecsd", hidden_act, w_down, preferred_element_type=jnp.float32)
    return down_act.astype(jnp.bfloat16)


def per_device_general(hidden, routes, w_router, w_gate, w_up, w_down):
    row_count = hidden.shape[0]
    top_count = routes.shape[1]
    experts = w_router.shape[1]
    slot_total = experts * CAP
    flat_routes = routes.reshape(-1)
    expert_ids = lax.iota(jnp.int32, experts)
    onehot = (flat_routes[:, None] == expert_ids[None, :]).astype(jnp.int32)
    running = jnp.cumsum(onehot, axis=0) - 1
    slot_index = jnp.sum(running * onehot, axis=1)
    target = flat_routes * CAP + slot_index
    placed = (target[:, None] == lax.iota(jnp.int32, slot_total)[None, :]).reshape(
        row_count, top_count, slot_total
    )
    dispatch_matrix = jnp.any(placed, axis=1).astype(jnp.bfloat16)
    full_rows, router_full = (
        lax.all_gather(hidden, ("tensor", "pair"), axis=1, tiled=True),
        lax.all_gather(w_router, ("tensor", "pair"), axis=0, tiled=True),
    )
    logits = jnp.dot(full_rows, router_full, preferred_element_type=jnp.float32)
    outbound = jnp.einsum(
        "rs,rd->sd", dispatch_matrix, full_rows, preferred_element_type=jnp.float32
    )
    outbound = outbound.astype(jnp.bfloat16).reshape(experts, 1, CAP, full_rows.shape[1])
    partial_value = experts_apply(
        lax.all_to_all(outbound, "expert", split_axis=0, concat_axis=1, tiled=True),
        w_gate,
        w_up,
        w_down,
    )
    scores = jax.nn.sigmoid(logits)
    route_hits = (routes[:, :, None] == expert_ids[None, None, :]).astype(jnp.float32)
    chosen = jnp.sum(scores[:, None, :] * route_hits, axis=2)
    gate_values = (route_scale * chosen / jnp.sum(chosen, axis=1, keepdims=True)).astype(
        jnp.bfloat16
    )
    summed = (
        lax.psum_scatter(partial_value, ("tensor", "pair"), scatter_dimension=3, tiled=True)
        .astype(jnp.float32)
        .astype(jnp.bfloat16)
    )
    returned = lax.all_to_all(summed, "expert", split_axis=1, concat_axis=0, tiled=True)
    expert_rows = returned.reshape(slot_total, returned.shape[3])
    combine_matrix = jnp.sum(placed.astype(jnp.bfloat16) * gate_values[:, :, None], axis=1)
    combined = jnp.dot(combine_matrix, expert_rows, preferred_element_type=jnp.float32)
    return (hidden.astype(jnp.float32) + combined).astype(jnp.bfloat16)


MESH = pl.DeviceIdType.MESH


def fused_kernel(
    n_expert,
    hidden_ref, routes_ref, router_ref, gate_hbm, up_hbm, down_hbm, out_ref,
    wg, wu, wd, xbuf, acc, act, logit_buf, gate_buf,
    ybuf, pair_in, xsum, x_in, zsum, z_in,
    w_sem, l_send, l_recv, g_send, g_recv,
    zx_send, zx_recv, px_send, px_recv, xx_send, xx_recv, dx_send, dx_recv,
    py_send, py_recv, xy_send, xy_recv, zy_send, zy_recv,
):
    rows, width = hidden_ref.shape
    local, depth, units = wg.shape
    half = depth // 2
    experts = router_ref.shape[1]
    grp, z = lax.axis_index("groups"), lax.axis_index("expert")
    t, p = lax.axis_index("tensor"), lax.axis_index("pair")
    z_at = [lax.rem(z + d, n_expert) for d in range(n_expert)]
    col = t * 2 + p

    def dev(zz, tt, pp):
        return (grp, zz, tt, pp)

    pair_dev, x_dev, diag_dev = dev(z, t, 1 - p), dev(z, 1 - t, p), dev(z, 1 - t, 1 - p)

    def row_ds(zz):
        return pl.ds(pl.multiple_of(zz * rows, 16), rows)

    def col_ds(tt, pp):
        return pl.ds(pl.multiple_of((tt * 2 + pp) * width, 128), width)

    def half_rows(h):
        tt = t if h == 0 else 1 - t
        return pl.ds(pl.multiple_of(tt * half, 128), half)

    def load_in(h, m, e):
        source, target = ((gate_hbm, wg), (up_hbm, wu))[m]
        where = half_rows(h)
        return pltpu.make_async_copy(source.at[e, where, :], target.at[e, where, :], w_sem.at[h * 2 + m, e])

    def load_down(e):
        return pltpu.make_async_copy(down_hbm.at[e], wd.at[e], w_sem.at[4, e])

    @pl.loop(0, local)
    def _(e):
        load_in(0, 0, e).start()
        load_in(0, 1, e).start()

    @pl.loop(0, local)
    def _(e):
        load_in(1, 0, e).start()
        load_in(1, 1, e).start()

    @pl.loop(0, local)
    def _(e):
        load_down(e).start()

    barrier = pltpu.get_barrier_semaphore()
    peers = [pair_dev, x_dev, diag_dev] + [dev(zz, t, p) for zz in z_at[1:]]
    for peer in peers:
        pl.semaphore_signal(barrier, inc=1, device_id=peer, device_id_type=MESH)
    pl.semaphore_wait(barrier, len(peers))

    sends = []

    def send(source, target, send_sem, recv_sem, device):
        copy = pltpu.make_async_remote_copy(
            src_ref=source, dst_ref=target, send_sem=send_sem, recv_sem=recv_sem,
            device_id=device, device_id_type=MESH,
        )
        copy.start()
        sends.append(copy)

    def arrived(target, send_sem, recv_sem, device):
        pltpu.make_async_remote_copy(
            src_ref=target, dst_ref=target, send_sem=send_sem, recv_sem=recv_sem,
            device_id=device, device_id_type=MESH,
        ).wait_recv()

    for d in range(n_expert - 1, 0, -1):
        send(hidden_ref, xbuf.at[row_ds(z), col_ds(t, p)], zx_send.at[d], zx_recv.at[z], dev(z_at[d], t, p))
    send(hidden_ref, xbuf.at[row_ds(z), col_ds(t, p)], xx_send.at[0], xx_recv.at[z], x_dev)
    send(hidden_ref, xbuf.at[row_ds(z), col_ds(t, p)], px_send.at[0], px_recv.at[z], pair_dev)
    xbuf[row_ds(z), col_ds(t, p)] = hidden_ref[...]

    logit_buf[col] = jnp.dot(hidden_ref[...], router_ref[...], preferred_element_type=jnp.float32)
    for i, peer in enumerate((pair_dev, x_dev, diag_dev)):
        send(logit_buf.at[col], logit_buf.at[col], l_send.at[i], l_recv.at[col], peer)

    for d in range(1, n_expert):
        zz = z_at[d]
        block = xbuf.at[row_ds(zz), col_ds(t, p)]
        arrived(block, zx_send.at[d], zx_recv.at[zz], dev(zz, t, p))
        send(block, block, xx_send.at[d], xx_recv.at[zz], x_dev)
        send(block, block, px_send.at[d], px_recv.at[zz], pair_dev)

    for i, (tt, pp) in enumerate(((t, 1 - p), (1 - t, p), (1 - t, 1 - p))):
        c = tt * 2 + pp
        arrived(logit_buf.at[c], l_send.at[i], l_recv.at[c], dev(z, tt, pp))
    logits = (logit_buf[0] + logit_buf[1]) + (logit_buf[2] + logit_buf[3])
    scores = 1.0 / (1.0 + jnp.exp(-logits))
    ids = lax.broadcasted_iota(jnp.int32, (rows, experts), 1)
    picks = routes_ref[...]
    chosen = jnp.zeros((rows, experts), jnp.float32)
    for k in range(picks.shape[1]):
        chosen = chosen + jnp.where(picks[:, k:k + 1] == ids, scores, 0.0)
    gates = route_scale * chosen / jnp.sum(chosen, axis=1, keepdims=True)
    gate_buf[z] = gates.astype(jnp.bfloat16).astype(jnp.float32)
    for d in range(1, n_expert):
        send(gate_buf.at[z], gate_buf.at[z], g_send.at[d], g_recv.at[z], dev(z_at[d], t, p))

    for d in range(n_expert):
        zz = z_at[d]
        arrived(xbuf.at[row_ds(zz), col_ds(t, 1 - p)], px_send.at[d], px_recv.at[zz], pair_dev)
    near = pl.ds(pl.multiple_of(t * half, 128), half)
    far = pl.ds(pl.multiple_of((1 - t) * half, 128), half)

    def first(e, carry):
        load_in(0, 0, e).wait()
        acc[0, e] = jnp.dot(xbuf[:, near], wg[e, half_rows(0), :], preferred_element_type=jnp.float32)
        load_in(0, 1, e).wait()
        acc[1, e] = jnp.dot(xbuf[:, near], wu[e, half_rows(0), :], preferred_element_type=jnp.float32)
        return carry

    step = local // n_expert
    for d in range(n_expert):
        lax.fori_loop(d * step, (d + 1) * step if d < n_expert - 1 else local, first, 0)
        zz = z_at[d]
        block = xbuf.at[row_ds(zz), col_ds(1 - t, p)]
        arrived(block, xx_send.at[d], xx_recv.at[zz], x_dev)
        send(block, block, dx_send.at[d], dx_recv.at[zz], pair_dev)
    for d in range(n_expert):
        zz = z_at[d]
        arrived(xbuf.at[row_ds(zz), col_ds(1 - t, 1 - p)], dx_send.at[d], dx_recv.at[zz], pair_dev)
    for d in range(1, n_expert):
        zz = z_at[d]
        arrived(gate_buf.at[zz], g_send.at[d], g_recv.at[zz], dev(zz, t, p))

    all_rows = n_expert * rows
    lanes = lax.broadcasted_iota(jnp.int32, (all_rows, experts), 1)

    def second(e, carry):
        load_in(1, 0, e).wait()
        gate_act = acc[0, e] + jnp.dot(xbuf[:, far], wg[e, half_rows(1), :], preferred_element_type=jnp.float32)
        load_in(1, 1, e).wait()
        up_act = acc[1, e] + jnp.dot(xbuf[:, far], wu[e, half_rows(1), :], preferred_element_type=jnp.float32)
        table = gate_buf[...].reshape(all_rows, experts)
        weight = jnp.sum(jnp.where(lanes == z * local + e, table, 0.0), axis=1, keepdims=True)
        value = gate_act / (1.0 + jnp.exp(-gate_act)) * up_act * weight
        act[:, pl.ds(pl.multiple_of(e * units, 128), units)] = value.astype(jnp.bfloat16)
        return carry

    lax.fori_loop(0, local, second, 0)

    @pl.loop(0, local)
    def _(e):
        load_down(e).wait()

    tile = 256 if half % 256 == 0 else 128
    for h in range(2):
        tt = 1 - t if h == 0 else t

        def down(n, carry):
            source = pl.ds(pl.multiple_of(tt * half + n * tile, 128), tile)
            weights = wd[:, :, source].reshape(local * units, tile)
            value = jnp.dot(act[...], weights, preferred_element_type=jnp.float32)
            ybuf[h, :, pl.ds(pl.multiple_of(n * tile, 128), tile)] = value.astype(jnp.bfloat16)
            return carry

        lax.fori_loop(0, half // tile, down, 0)
        other = pl.ds(pl.multiple_of((1 - p) * width, 128), width)
        send(ybuf.at[h, :, other], pair_in.at[h], py_send.at[h], py_recv.at[h], pair_dev)
        if h == 0:
            continue
        mine = pl.ds(pl.multiple_of(p * width, 128), width)
        arrived(pair_in.at[0], py_send.at[0], py_recv.at[0], pair_dev)
        for d in [*range(1, n_expert), 0]:
            zz = z_at[d]
            part = ybuf[0, row_ds(zz), mine].astype(jnp.float32) + pair_in[0, row_ds(zz), :].astype(jnp.float32)
            xsum[zz] = part.astype(jnp.bfloat16)
            send(xsum.at[zz], x_in.at[zz], xy_send.at[d], xy_recv.at[zz], x_dev)
        arrived(pair_in.at[1], py_send.at[1], py_recv.at[1], pair_dev)

    def own_sum(zz, d):
        arrived(x_in.at[zz], xy_send.at[d], xy_recv.at[zz], x_dev)
        part = ybuf[1, row_ds(zz), mine].astype(jnp.float32) + pair_in[1, row_ds(zz), :].astype(jnp.float32)
        return part + x_in[zz].astype(jnp.float32)

    for d in range(1, n_expert):
        zz = z_at[d]
        zsum[zz] = own_sum(zz, d).astype(jnp.bfloat16)
        send(zsum.at[zz], z_in.at[z], zy_send.at[d], zy_recv.at[z], dev(zz, t, p))
    total = hidden_ref[...].astype(jnp.float32) + own_sum(z, 0)
    for d in range(n_expert - 1, 0, -1):
        zz = z_at[d]
        arrived(z_in.at[zz], zy_send.at[d], zy_recv.at[zz], dev(zz, t, p))
        total = total + z_in[zz].astype(jnp.float32)
    out_ref[...] = total.astype(jnp.bfloat16)
    for copy in sends:
        copy.wait_send()


def fused(n_expert, hidden, routes, w_router, w_gate, w_up, w_down):
    rows, width = hidden.shape
    local, depth, units = w_gate.shape
    experts = w_router.shape[1]
    all_rows = n_expert * rows
    half = depth // 2
    vmem = pl.BlockSpec(memory_space=pltpu.VMEM)
    far = pl.BlockSpec(memory_space=pl.ANY)
    bf16, f32 = jnp.bfloat16, jnp.float32

    def dma(*shape):
        return pltpu.SemaphoreType.DMA(shape)

    n = n_expert
    return pl.pallas_call(
        functools.partial(fused_kernel, n_expert),
        out_shape=jax.ShapeDtypeStruct((rows, width), bf16),
        in_specs=[vmem, vmem, vmem, far, far, far],
        out_specs=vmem,
        scratch_shapes=[
            pltpu.VMEM((local, depth, units), bf16),
            pltpu.VMEM((local, depth, units), bf16),
            pltpu.VMEM((local, units, depth), bf16),
            pltpu.VMEM((all_rows, depth), bf16),
            pltpu.VMEM((2, local, all_rows, units), f32),
            pltpu.VMEM((all_rows, local * units), bf16),
            pltpu.VMEM((4, rows, experts), f32),
            pltpu.VMEM((n, rows, experts), f32),
            pltpu.VMEM((2, all_rows, half), bf16),
            pltpu.VMEM((2, all_rows, width), bf16),
            pltpu.VMEM((n, rows, width), bf16),
            pltpu.VMEM((n, rows, width), bf16),
            pltpu.VMEM((n, rows, width), bf16),
            pltpu.VMEM((n, rows, width), bf16),
            dma(5, local), dma(3), dma(4), dma(n), dma(n),
            dma(n), dma(n), dma(n), dma(n), dma(n), dma(n), dma(n), dma(n),
            dma(2), dma(2), dma(n), dma(n), dma(n), dma(n),
        ],
        compiler_params=pltpu.CompilerParams(
            collective_id=0, has_side_effects=True, vmem_limit_bytes=58 * 1024 * 1024
        ),
        cost_estimate=pl.CostEstimate(
            flops=6 * all_rows * local * depth * units,
            bytes_accessed=6 * local * depth * units,
            transcendentals=all_rows * local * units,
        ),
    )(hidden, routes, w_router, w_gate, w_up, w_down)


def per_device(n_expert, n_tensor, n_pair, hidden, routes, w_router, w_gate, w_up, w_down):
    rows, width = hidden.shape
    local, depth, units = w_gate.shape
    held = 2 * 3 * local * depth * units
    fits = held <= 44 * 1024 * 1024 and local % n_expert == 0
    if n_tensor == 2 and n_pair == 2 and width % 128 == 0 and units % 128 == 0 and rows % 16 == 0 and fits:
        return fused(n_expert, hidden, routes, w_router, w_gate, w_up, w_down)
    return per_device_general(hidden, routes, w_router, w_gate, w_up, w_down)


def solution(mesh):
    in_specs = (
        P(("groups", "expert"), ("tensor", "pair")),
        P(("groups", "expert"), None),
        P(("tensor", "pair"), None),
        P("expert", None, ("tensor", "pair")),
        P("expert", None, ("tensor", "pair")),
        P("expert", ("tensor", "pair"), None),
    )
    out_specs = P(("groups", "expert"), ("tensor", "pair"))
    return jax.shard_map(
        functools.partial(per_device, mesh.shape["expert"], mesh.shape["tensor"], mesh.shape["pair"]),
        mesh=mesh, in_specs=in_specs, out_specs=out_specs, check_vma=False
    )
```

```python
import functools

import jax
import jax.numpy as jnp
from jax import lax
from jax.experimental import pallas as pl
from jax.experimental.pallas import tpu as pltpu
from jax.sharding import PartitionSpec as P

CAP = 18


route_scale = 2.5


def experts_apply(received, w_gate, w_up, w_down):
    gate_act = jnp.einsum("ecsd,edf->ecsf", received, w_gate, preferred_element_type=jnp.float32)
    up_act = jnp.einsum("ecsd,edf->ecsf", received, w_up, preferred_element_type=jnp.float32)
    hidden_act = (jax.nn.silu(gate_act) * up_act).astype(jnp.bfloat16)
    down_act = jnp.einsum("ecsf,efd->ecsd", hidden_act, w_down, preferred_element_type=jnp.float32)
    return down_act.astype(jnp.bfloat16)


def per_device_general(hidden, routes, w_router, w_gate, w_up, w_down):
    row_count = hidden.shape[0]
    top_count = routes.shape[1]
    experts = w_router.shape[1]
    slot_total = experts * CAP
    flat_routes = routes.reshape(-1)
    expert_ids = lax.iota(jnp.int32, experts)
    onehot = (flat_routes[:, None] == expert_ids[None, :]).astype(jnp.int32)
    running = jnp.cumsum(onehot, axis=0) - 1
    slot_index = jnp.sum(running * onehot, axis=1)
    target = flat_routes * CAP + slot_index
    placed = (target[:, None] == lax.iota(jnp.int32, slot_total)[None, :]).reshape(
        row_count, top_count, slot_total
    )
    dispatch_matrix = jnp.any(placed, axis=1).astype(jnp.bfloat16)
    full_rows, router_full = (
        lax.all_gather(hidden, ("tensor", "pair"), axis=1, tiled=True),
        lax.all_gather(w_router, ("tensor", "pair"), axis=0, tiled=True),
    )
    logits = jnp.dot(full_rows, router_full, preferred_element_type=jnp.float32)
    outbound = jnp.einsum(
        "rs,rd->sd", dispatch_matrix, full_rows, preferred_element_type=jnp.float32
    )
    outbound = outbound.astype(jnp.bfloat16).reshape(experts, 1, CAP, full_rows.shape[1])
    partial_value = experts_apply(
        lax.all_to_all(outbound, "expert", split_axis=0, concat_axis=1, tiled=True),
        w_gate,
        w_up,
        w_down,
    )
    scores = jax.nn.sigmoid(logits)
    route_hits = (routes[:, :, None] == expert_ids[None, None, :]).astype(jnp.float32)
    chosen = jnp.sum(scores[:, None, :] * route_hits, axis=2)
    gate_values = (route_scale * chosen / jnp.sum(chosen, axis=1, keepdims=True)).astype(
        jnp.bfloat16
    )
    summed = (
        lax.psum_scatter(partial_value, ("tensor", "pair"), scatter_dimension=3, tiled=True)
        .astype(jnp.float32)
        .astype(jnp.bfloat16)
    )
    returned = lax.all_to_all(summed, "expert", split_axis=1, concat_axis=0, tiled=True)
    expert_rows = returned.reshape(slot_total, returned.shape[3])
    combine_matrix = jnp.sum(placed.astype(jnp.bfloat16) * gate_values[:, :, None], axis=1)
    combined = jnp.dot(combine_matrix, expert_rows, preferred_element_type=jnp.float32)
    return (hidden.astype(jnp.float32) + combined).astype(jnp.bfloat16)


MESH = pl.DeviceIdType.MESH


def fused_kernel(
    n_expert,
    hidden_ref, routes_ref, router_ref, gate_hbm, up_hbm, down_hbm, out_ref,
    wg, wu, wd, xbuf, acc, act, logit_buf, gate_buf,
    ybuf, pair_in, xsum, x_in, zsum, z_in,
    w_sem, l_send, l_recv, g_send, g_recv,
    zx_send, zx_recv, px_send, px_recv, xx_send, xx_recv, dx_send, dx_recv,
    py_send, py_recv, xy_send, xy_recv, zy_send, zy_recv,
):
    rows, width = hidden_ref.shape
    local, depth, units = wg.shape
    half = depth // 2
    experts = router_ref.shape[0]
    grp, z = lax.axis_index("groups"), lax.axis_index("expert")
    t, p = lax.axis_index("tensor"), lax.axis_index("pair")
    z_at = [z, z + 1 - 2 * lax.rem(z, 2), lax.rem(z + 2, 4), 3 - z]
    col = t * 2 + p

    def dev(zz, tt, pp):
        return (grp, zz, tt, pp)

    pair_dev, x_dev, diag_dev = dev(z, t, 1 - p), dev(z, 1 - t, p), dev(z, 1 - t, 1 - p)

    def row_ds(zz):
        return pl.ds(pl.multiple_of(zz * rows, 16), rows)

    def col_ds(tt, pp):
        return pl.ds(pl.multiple_of((tt * 2 + pp) * width, 128), width)

    def half_rows(h):
        tt = t if h == 0 else 1 - t
        return pl.ds(pl.multiple_of(tt * half, 128), half)

    def load_in(h, m, e):
        source, target = ((gate_hbm, wg), (up_hbm, wu))[m]
        where = half_rows(h)
        return pltpu.make_async_copy(source.at[e, where, :], target.at[e, where, :], w_sem.at[h * 2 + m, e])

    def load_down(e):
        return pltpu.make_async_copy(down_hbm.at[e], wd.at[e], w_sem.at[4, e])

    @pl.loop(0, local)
    def _(e):
        load_in(0, 0, e).start()
        load_in(0, 1, e).start()

    @pl.loop(0, local)
    def _(e):
        load_in(1, 0, e).start()
        load_in(1, 1, e).start()

    @pl.loop(0, local)
    def _(e):
        load_down(e).start()

    barrier = pltpu.get_barrier_semaphore()
    peers = [pair_dev, x_dev, diag_dev] + [dev(zz, t, p) for zz in z_at[1:]]
    for peer in peers:
        pl.semaphore_signal(barrier, inc=1, device_id=peer, device_id_type=MESH)
    pl.semaphore_wait(barrier, len(peers))

    sends = []

    def send(source, target, send_sem, recv_sem, device):
        copy = pltpu.make_async_remote_copy(
            src_ref=source, dst_ref=target, send_sem=send_sem, recv_sem=recv_sem,
            device_id=device, device_id_type=MESH,
        )
        copy.start()
        sends.append(copy)

    def arrived(target, send_sem, recv_sem, device):
        pltpu.make_async_remote_copy(
            src_ref=target, dst_ref=target, send_sem=send_sem, recv_sem=recv_sem,
            device_id=device, device_id_type=MESH,
        ).wait_recv()

    send(hidden_ref, xbuf.at[row_ds(z), col_ds(t, p)], xx_send.at[0], xx_recv.at[z], x_dev)
    send(hidden_ref, xbuf.at[row_ds(z), col_ds(t, p)], px_send.at[0], px_recv.at[z], pair_dev)
    for d in range(1, n_expert):
        send(hidden_ref, xbuf.at[row_ds(z), col_ds(t, p)], zx_send.at[d], zx_recv.at[z], dev(z_at[d], t, p))
    xbuf[row_ds(z), col_ds(t, p)] = hidden_ref[...]

    logit_buf[col] = lax.dot_general(
        router_ref[...], hidden_ref[...], (((1,), (1,)), ((), ())), preferred_element_type=jnp.float32
    )
    for i, peer in enumerate((pair_dev, x_dev, diag_dev)):
        send(logit_buf.at[col], logit_buf.at[col], l_send.at[i], l_recv.at[col], peer)

    for d in range(1, n_expert):
        zz = z_at[d]
        block = xbuf.at[row_ds(zz), col_ds(t, p)]
        arrived(block, zx_send.at[d], zx_recv.at[zz], dev(zz, t, p))
        send(block, block, xx_send.at[d], xx_recv.at[zz], x_dev)
        send(block, block, px_send.at[d], px_recv.at[zz], pair_dev)

    for i, (tt, pp) in enumerate(((t, 1 - p), (1 - t, p), (1 - t, 1 - p))):
        c = tt * 2 + pp
        arrived(logit_buf.at[c], l_send.at[i], l_recv.at[c], dev(z, tt, pp))
    logits = (logit_buf[0] + logit_buf[1]) + (logit_buf[2] + logit_buf[3])
    scores = 1.0 / (1.0 + jnp.exp(-logits))
    ids = lax.broadcasted_iota(jnp.int32, (experts, rows), 0)
    picks = routes_ref[...]
    chosen = jnp.zeros((experts, rows), jnp.float32)
    for k in range(picks.shape[0]):
        chosen = chosen + jnp.where(picks[k:k + 1, :] == ids, scores, 0.0)
    gates = route_scale * chosen / jnp.sum(chosen, axis=0, keepdims=True)
    gate_buf[z] = jnp.transpose(gates.astype(jnp.bfloat16).astype(jnp.float32))
    for d in range(1, n_expert):
        send(gate_buf.at[z], gate_buf.at[z], g_send.at[d], g_recv.at[z], dev(z_at[d], t, p))

    for d in range(n_expert):
        zz = z_at[d]
        arrived(xbuf.at[row_ds(zz), col_ds(t, 1 - p)], px_send.at[d], px_recv.at[zz], pair_dev)
    near = pl.ds(pl.multiple_of(t * half, 128), half)
    far = pl.ds(pl.multiple_of((1 - t) * half, 128), half)

    def first(e, carry):
        load_in(0, 0, e).wait()
        acc[0, e] = jnp.dot(xbuf[:, near], wg[e, half_rows(0), :], preferred_element_type=jnp.float32)
        load_in(0, 1, e).wait()
        acc[1, e] = jnp.dot(xbuf[:, near], wu[e, half_rows(0), :], preferred_element_type=jnp.float32)
        return carry

    step = local // n_expert
    for d in range(n_expert):
        lax.fori_loop(d * step, (d + 1) * step if d < n_expert - 1 else local, first, 0, unroll=True)
        zz = z_at[d]
        block = xbuf.at[row_ds(zz), col_ds(1 - t, p)]
        arrived(block, xx_send.at[d], xx_recv.at[zz], x_dev)
        send(block, block, dx_send.at[d], dx_recv.at[zz], pair_dev)
    for d in range(n_expert):
        zz = z_at[d]
        arrived(xbuf.at[row_ds(zz), col_ds(1 - t, 1 - p)], dx_send.at[d], dx_recv.at[zz], pair_dev)
    for d in range(1, n_expert):
        zz = z_at[d]
        arrived(gate_buf.at[zz], g_send.at[d], g_recv.at[zz], dev(zz, t, p))

    all_rows = n_expert * rows
    lanes = lax.broadcasted_iota(jnp.int32, (all_rows, experts), 1)

    def second(e, carry):
        load_in(1, 0, e).wait()
        gate_act = acc[0, e] + jnp.dot(xbuf[:, far], wg[e, half_rows(1), :], preferred_element_type=jnp.float32)
        load_in(1, 1, e).wait()
        up_act = acc[1, e] + jnp.dot(xbuf[:, far], wu[e, half_rows(1), :], preferred_element_type=jnp.float32)
        table = gate_buf[...].reshape(all_rows, experts)
        weight = jnp.sum(jnp.where(lanes == z * local + e, table, 0.0), axis=1, keepdims=True)
        value = gate_act / (1.0 + jnp.exp(-gate_act)) * up_act * weight
        act[:, pl.ds(pl.multiple_of(e * units, 128), units)] = value.astype(jnp.bfloat16)
        return carry

    lax.fori_loop(0, local, second, 0, unroll=True)

    @pl.loop(0, local)
    def _(e):
        load_down(e).wait()

    def down(k, tt, pp, start, size):
        for begin in range(start, start + size, 256):
            count = min(256, start + size - begin)
            source = pl.ds(pl.multiple_of((tt * 2 + pp) * width + begin, 128), count)
            weights = wd[:, :, source].reshape(local * units, count)
            value = jnp.dot(act[...], weights, preferred_element_type=jnp.float32)
            ybuf[k, :, pl.ds(begin, count)] = value.astype(jnp.bfloat16)

    cut = width // 256 * 128 + 128 if width % 256 else width // 2
    parts = ((0, cut), (cut, width - cut))

    def pair_sum(h, i, zz):
        where = pl.ds(*parts[i])
        return ybuf[2 * h + 1, row_ds(zz), where].astype(jnp.float32) + pair_in[h, row_ds(zz), where].astype(jnp.float32)

    for h in range(2):
        tt = 1 - t if h == 0 else t
        for i, (start, size) in enumerate(parts):
            where = pl.ds(start, size)
            down(2 * h, tt, 1 - p, start, size)
            landing = pair_in.at[h, :, where]
            send(ybuf.at[2 * h, :, where], landing, py_send.at[h, i], py_recv.at[h, i], pair_dev)
            down(2 * h + 1, tt, p, start, size)
            arrived(landing, py_send.at[h, i], py_recv.at[h, i], pair_dev)
            if h == 1:
                continue
            for d in (1, 2, 3, 0):
                zz = z_at[d]
                xsum[zz, :, where] = pair_sum(0, i, zz).astype(jnp.bfloat16)
                send(xsum.at[zz, :, where], x_in.at[zz, :, where], xy_send.at[i, d], xy_recv.at[i, zz], x_dev)

    def own_sum(zz, d, i):
        where = pl.ds(*parts[i])
        arrived(x_in.at[zz, :, where], xy_send.at[i, d], xy_recv.at[i, zz], x_dev)
        return pair_sum(1, i, zz) + x_in[zz, :, where].astype(jnp.float32)

    for i in range(2):
        where = pl.ds(*parts[i])
        for d in range(1, n_expert):
            zz = z_at[d]
            zsum[zz, :, where] = own_sum(zz, d, i).astype(jnp.bfloat16)
            send(zsum.at[zz, :, where], z_in.at[z, :, where], zy_send.at[i, d], zy_recv.at[i, z], dev(zz, t, p))
    for i in range(2):
        where = pl.ds(*parts[i])
        total = hidden_ref[:, where].astype(jnp.float32) + own_sum(z, 0, i)
        for d in range(1, n_expert):
            zz = z_at[d]
            arrived(z_in.at[zz, :, where], zy_send.at[i, d], zy_recv.at[i, zz], dev(zz, t, p))
            total = total + z_in[zz, :, where].astype(jnp.float32)
        out_ref[:, where] = total.astype(jnp.bfloat16)
    for copy in sends:
        copy.wait_send()


def fused(n_expert, hidden, routes, w_router, w_gate, w_up, w_down):
    rows, width = hidden.shape
    local, depth, units = w_gate.shape
    experts = w_router.shape[1]
    all_rows = n_expert * rows
    half = depth // 2
    vmem = pl.BlockSpec(memory_space=pltpu.VMEM)
    far = pl.BlockSpec(memory_space=pl.ANY)
    bf16, f32 = jnp.bfloat16, jnp.float32

    def dma(*shape):
        return pltpu.SemaphoreType.DMA(shape)

    n = n_expert
    return pl.pallas_call(
        functools.partial(fused_kernel, n_expert),
        out_shape=jax.ShapeDtypeStruct((rows, width), bf16),
        in_specs=[vmem, vmem, vmem, far, far, far],
        out_specs=vmem,
        scratch_shapes=[
            pltpu.VMEM((local, depth, units), bf16),
            pltpu.VMEM((local, depth, units), bf16),
            pltpu.VMEM((local, units, depth), bf16),
            pltpu.VMEM((all_rows, depth), bf16),
            pltpu.VMEM((2, local, all_rows, units), f32),
            pltpu.VMEM((all_rows, local * units), bf16),
            pltpu.VMEM((4, experts, rows), f32),
            pltpu.VMEM((n, rows, experts), f32),
            pltpu.VMEM((4, all_rows, width), bf16),
            pltpu.VMEM((2, all_rows, width), bf16),
            pltpu.VMEM((n, rows, width), bf16),
            pltpu.VMEM((n, rows, width), bf16),
            pltpu.VMEM((n, rows, width), bf16),
            pltpu.VMEM((n, rows, width), bf16),
            dma(5, local), dma(3), dma(4), dma(n), dma(n),
            dma(n), dma(n), dma(n), dma(n), dma(n), dma(n), dma(n), dma(n),
            dma(2, 2), dma(2, 2), dma(2, n), dma(2, n), dma(2, n), dma(2, n),
        ],
        compiler_params=pltpu.CompilerParams(
            collective_id=0, has_side_effects=True, vmem_limit_bytes=58 * 1024 * 1024
        ),
        cost_estimate=pl.CostEstimate(
            flops=6 * all_rows * local * depth * units,
            bytes_accessed=6 * local * depth * units,
            transcendentals=all_rows * local * units,
        ),
    )(hidden, routes.T, w_router.T, w_gate, w_up, w_down)


def per_device(n_expert, n_tensor, n_pair, hidden, routes, w_router, w_gate, w_up, w_down):
    rows, width = hidden.shape
    local, depth, units = w_gate.shape
    held = 2 * 3 * local * depth * units
    fits = held <= 44 * 1024 * 1024 and n_expert == 4 and local % n_expert == 0
    if n_tensor == 2 and n_pair == 2 and width % 128 == 0 and units % 128 == 0 and rows % 16 == 0 and fits:
        return fused(n_expert, hidden, routes, w_router, w_gate, w_up, w_down)
    return per_device_general(hidden, routes, w_router, w_gate, w_up, w_down)


def solution(mesh):
    in_specs = (
        P(("groups", "expert"), ("tensor", "pair")),
        P(("groups", "expert"), None),
        P(("tensor", "pair"), None),
        P("expert", None, ("tensor", "pair")),
        P("expert", None, ("tensor", "pair")),
        P("expert", ("tensor", "pair"), None),
    )
    out_specs = P(("groups", "expert"), ("tensor", "pair"))
    return jax.shard_map(
        functools.partial(per_device, mesh.shape["expert"], mesh.shape["tensor"], mesh.shape["pair"]),
        mesh=mesh, in_specs=in_specs, out_specs=out_specs, check_vma=False
    )
```
